512 devices in a mesh: vocab: 64 (over z, y), inner: 2 (over core), rep: 4 (over x).
Axes of the slice: x: 4, y: 8, z: 8, core: 2. Of those that a mesh axis runs over, the one named last changes fastest.
Arguments:
- teacher_hidden: bfloat16 [512, 4608], P('rep', 'inner'), may hold values from -6 to 6
- teacher_embed: bfloat16 [131072, 4608], P(('vocab', 'rep'), 'inner'), may hold values from -0.87890625 to 0.87890625
- student_hidden: bfloat16 [512, 3584], P('rep', 'inner'), may hold values from -6 to 6
- student_embed: bfloat16 [131072, 3584], P(('vocab', 'rep'), 'inner'), may hold values from -1 to 1
- labels: int32 [512], replicated, may hold values from 0 to 131071, as said below
- loss_mask: int32 [512], replicated, may hold values 0 or 1
Outputs:
- loss: float32 [], replicated
- hidden_grad: bfloat16 [512, 3584], P('rep', 'inner')
The draws below stay inside these ranges and needn't reach their ends.
Inputs may be any that keep to these rules, and one draw needn't show every extreme that they name: `labels`: split the tokens into quarters of 128 rows in order, and the vocabulary into blocks of 512 entries numbered vocab index times 4 plus rep index. The ids of the tokens of quarter r lie only in blocks with rep index r, and every vocab index has at least one token of the quarter whose id lies in its block.
All inputs are finite; a program needn't handle non-finite values.
Results may differ from the reference program's by a relative error of at most 0.009.
Values may be sent and summed in bfloat16 or wider, within the bound.
A program may use at most 64 MiB of HBM per device.

```python
import jax
import jax.numpy as jnp
from jax import lax

V = 131072
DT = 4608
DS = 3584
TOK = 512
N_VOCAB = 64
N_REP = 4


def draw_labels(key, part):
    key = jax.random.fold_in(key, 7)
    order_key = jax.random.fold_in(key, 1)
    offset_key = jax.random.fold_in(key, 2)
    quarter_rows = TOK // N_REP
    shard_width = V // (N_VOCAB * N_REP)
    raw_scores = jax.random.randint(order_key, (N_REP, quarter_rows), 0, 1 << 20, dtype=jnp.int32)
    distinct = raw_scores * quarter_rows + jnp.arange(quarter_rows, dtype=jnp.int32)[None, :]
    ranks = jnp.argsort(distinct, axis=1, stable=True).astype(jnp.int32)
    vocab_index = ranks % N_VOCAB
    rep_index = jnp.arange(N_REP, dtype=jnp.int32)[:, None]
    shard_number = vocab_index * N_REP + rep_index
    offsets = jax.random.randint(offset_key, (N_REP, quarter_rows), 0, shard_width, dtype=jnp.int32)
    return (shard_number * shard_width + offsets).reshape(TOK).astype(jnp.int32)


def set_ends(array, key, smallest, largest):
    longest = array.shape.index(max(array.shape))
    spots = []
    for shift in (0, 1):
        where = [jax.random.randint(jax.random.fold_in(key, axis), (), 0, length) for axis, length in enumerate(array.shape)]
        where[longest] = (where[longest] + shift) % array.shape[longest]
        spots.append(tuple(where))
    return array.at[spots[0]].set(smallest).at[spots[1]].set(largest)


def levels(key, dims, cuts, least, high):
    factor_of, own = 1.0, jax.random.fold_in(key, 6)
    for dim, blocks in cuts:
        heights = jnp.exp(jax.random.uniform(jax.random.fold_in(own, dim), (blocks,), jnp.float32, least / len(cuts), high / len(cuts)))
        factor_of = factor_of * jnp.repeat(heights, dims[dim] // blocks).reshape([-1 if axis == dim else 1 for axis in range(len(dims))])
    return factor_of


def centred(stream_key, shape, scale, bound, cuts=(), held_as=jnp.bfloat16):
    result = jax.random.normal(stream_key, shape, jnp.float32) * scale
    if len(cuts) > 0:
        result = levels(stream_key, shape, cuts, -0.22, 0.18) * result
    return jnp.clip(result, min=-bound, max=bound).astype(held_as)


def setup_inputs(seed: int = 0) -> dict:
    seeds = jax.random.split(jax.random.key(seed), 7)
    return {
        "teacher_hidden": centred(seeds[0], (TOK, DT), 1.0, 6.0, ((0, 4), (1, 2))),
        "teacher_embed": centred(seeds[1], (V, DT), 0.11, 0.87890625, ((0, 256), (1, 2))),
        "student_hidden": centred(seeds[2], (TOK, DS), 1.0, 6.0, ((0, 4), (1, 2))),
        "student_embed": centred(seeds[3], (V, DS), 0.125, 1.0, ((0, 256), (1, 2))),
        "labels": draw_labels(jax.random.fold_in(seeds[6], 71), 0),
        "loss_mask": set_ends((jax.random.randint(seeds[5], (TOK,), 0, 5) < 4).astype(jnp.int32), jax.random.fold_in(seeds[5], 1), 0, 1),
    }


LOGIT_CAP = 30.0
SOFTMAX_TEMPER = 2.0
SOFT_LOSS_WEIGHT = 0.5


def capped(scores):
    bounded = jnp.tanh(scores / LOGIT_CAP)
    return LOGIT_CAP * bounded, bounded


def reference(teacher_hidden, teacher_embed, student_hidden, student_embed, labels, loss_mask):
    teacher_scores = jnp.dot(teacher_hidden, teacher_embed.T, preferred_element_type=jnp.float32)
    teacher_logit_rows = capped(teacher_scores)[0]
    teacher_probability = jnp.exp(teacher_logit_rows / SOFTMAX_TEMPER).astype(jnp.bfloat16)
    teacher_exp_values = lax.optimization_barrier(teacher_probability).astype(jnp.float32)
    student_scores = jnp.dot(student_hidden, student_embed.T, preferred_element_type=jnp.float32)
    student_logit_rows, bounded = capped(student_scores)
    soft_loss_terms = jnp.exp(student_logit_rows / SOFTMAX_TEMPER)
    hard_loss_terms = jnp.exp(student_logit_rows)
    columns = jnp.arange(V, dtype=jnp.int32)
    target_labels = (columns[None, :] == labels[:, None]).astype(jnp.float32)
    teacher_partition = jnp.sum(teacher_exp_values, axis=1)
    soft_loss_total = jnp.sum(soft_loss_terms, axis=1)
    hard_loss_total = jnp.sum(hard_loss_terms, axis=1)
    cross_entropy = jnp.sum(teacher_exp_values * student_logit_rows, axis=1) / SOFTMAX_TEMPER
    label_logit_value = jnp.sum(target_labels * student_logit_rows, axis=1)
    weight_matrix = loss_mask.astype(jnp.float32)
    token_losses = SOFT_LOSS_WEIGHT * SOFTMAX_TEMPER * SOFTMAX_TEMPER * (jnp.log(soft_loss_total) - cross_entropy / teacher_partition) + (1.0 - SOFT_LOSS_WEIGHT) * (jnp.log(hard_loss_total) - label_logit_value)
    loss = jnp.sum(weight_matrix * token_losses) / jnp.maximum(jnp.sum(weight_matrix), 1.0)
    capped_slope = weight_matrix[:, None] * (SOFT_LOSS_WEIGHT * SOFTMAX_TEMPER * (soft_loss_terms / soft_loss_total[:, None] - teacher_exp_values / teacher_partition[:, None]) + (1.0 - SOFT_LOSS_WEIGHT) * (hard_loss_terms / hard_loss_total[:, None] - target_labels))
    logit_grad = (capped_slope * (1.0 - bounded * bounded)).astype(jnp.bfloat16)
    hidden_grad = jnp.dot(logit_grad, student_embed, preferred_element_type=jnp.float32).astype(jnp.bfloat16)
    return loss, hidden_grad
```

```python
import jax
import jax.numpy as jnp
from jax import lax
from jax.experimental import pallas as pl
from jax.experimental.pallas import tpu as pltpu
from jax.sharding import PartitionSpec as P

MESH = pl.DeviceIdType.MESH
CAP = 30.0
NX, NY, NZ = 4, 8, 8
TOK, DT, DS, VB = 512, 2304, 1792, 512
HALF = TOK // 2
QUARTER = TOK // NX
CXY, CYX = 512, 384
CA = CXY + CYX
F32, BF16 = jnp.float32, jnp.bfloat16


def nt(left, right):
    return lax.dot_general(left, right, (((1,), (1,)), ((), ())), preferred_element_type=F32)


def body(
    th, te, sh, se, lab, msk, loss_ref, out_ref,
    thg, shg, tev, sev,
    tsend, trecv, town, ssend, srecv, sown,
    wts, soft, bnd, labc, mskc, stat, statc, sx, sy, sz, lbuf, lrecv,
    gfull, gx, gy, gz, rx, ry, rz, hxy, hxz, r2y, r2z, hx2, r2x, a3, b3, ra, rb, outv,
    lsem, gs, gr, cs, cr, xs, xr, ys, yr, zs, zr, x1s, x1r, y1s, y1r, z1s, z1r,
    x2s, x2r, y2s, y2r, z2s, z2r, az, azr, by, byr, ay, ayr, bz, bzr,
):
    v = lax.axis_index("vocab")
    c = lax.axis_index("inner")
    x = lax.axis_index("rep")
    z, y = v // NY, v % NY

    def xi(k):
        return lax.rem(x + k, NX)

    def yi(k):
        return lax.rem(y + k, NY)

    def zi(k):
        return lax.rem(z + k, NZ)

    def xp(k):
        return (v, c, xi(k))

    def yp(k):
        return (z * NY + yi(k), c, x)

    def zp(k):
        return (zi(k) * NY + y, c, x)

    cp = (v, 1 - c, x)

    def send(src, dst, ssem, rsem, to):
        copy = pltpu.make_async_remote_copy(
            src_ref=src, dst_ref=dst, send_sem=ssem, recv_sem=rsem, device_id=to, device_id_type=MESH
        )
        copy.start()
        return copy

    def arrive(copies):
        for copy in copies:
            copy.wait_recv()

    def leave(copies):
        for copy in copies:
            copy.wait_send()

    loads = [
        pltpu.make_async_copy(se, sev, lsem.at[0]),
        pltpu.make_async_copy(te, tev, lsem.at[1]),
        pltpu.make_async_copy(sh, shg.at[x], lsem.at[2]),
        pltpu.make_async_copy(th, thg.at[x], lsem.at[3]),
    ]
    for load in loads:
        load.start()

    barrier = pltpu.get_barrier_semaphore()
    for k in range(1, NX):
        pl.semaphore_signal(barrier, inc=1, device_id=xp(k), device_id_type=MESH)
    for k in range(1, NY):
        pl.semaphore_signal(barrier, inc=1, device_id=yp(k), device_id_type=MESH)
    for k in range(1, NZ):
        pl.semaphore_signal(barrier, inc=1, device_id=zp(k), device_id_type=MESH)
    pl.semaphore_signal(barrier, inc=1, device_id=cp, device_id_type=MESH)
    pl.semaphore_wait(barrier, NX + NY + NZ - 2)

    sgather = [send(sh, shg.at[x], gs.at[k], gr.at[k], xp(k)) for k in range(1, NX)]
    tgather = [send(th, thg.at[x], gs.at[NX + k], gr.at[NX + k], xp(k)) for k in range(1, NX)]

    labc[...] = jnp.transpose(jnp.broadcast_to(lab[pl.ds(c, 1), :].astype(F32), (128, HALF)))
    maskrow = msk[pl.ds(c, 1), :].astype(F32)
    mskc[...] = jnp.transpose(jnp.broadcast_to(maskrow, (128, HALF)))

    def scores(gathered, table, depth, sent, own):
        def rows(which):
            return gathered[pl.ds(2 * which, 2)].reshape(HALF, depth)

        for n in range(0, VB, 256):
            sent[:, n : n + 256] = nt(rows(1 - c), table[n : n + 256, :]).astype(sent.dtype)

        def rest():
            for n in range(0, VB, 256):
                own[:, n : n + 256] = nt(rows(c), table[n : n + 256, :])

        return rest

    loads[0].wait()
    loads[2].wait()
    arrive(sgather)
    rest = scores(shg, sev, DS, ssend, sown)
    score_s = send(ssend, srecv, cs.at[0], cr.at[0], cp)
    rest()

    score_s.wait_recv()
    lane = lax.broadcasted_iota(jnp.int32, (32, 128), 1)
    column = lax.broadcasted_iota(jnp.int32, (32, VB), 1) + (v * NX + x) * VB
    columnf = column.astype(F32)

    def student(i, carry):
        at = pl.ds(pl.multiple_of(i * 32, 32), 32)
        b = jnp.tanh((sown[at, :] + srecv[at, :]) / CAP)
        s = jnp.exp((CAP / 2) * b)
        bnd[at, :] = b
        soft[at, :] = s
        hit = jnp.where(columnf == labc[at, 0:1], b, 0.0)
        total = jnp.sum(s, axis=1, keepdims=True)
        hard = jnp.sum(s * s, axis=1, keepdims=True)
        label = CAP * jnp.sum(hit, axis=1, keepdims=True)
        stat[at, :] = jnp.where(lane == 1, total, jnp.where(lane == 2, hard, jnp.where(lane == 4, label, 0.0)))
        return carry

    lax.fori_loop(0, HALF // 32, student, 0)

    loads[1].wait()
    loads[3].wait()
    arrive(tgather)
    rest = scores(thg, tev, DT, tsend, town)
    score_t = send(tsend, trecv, cs.at[1], cr.at[1], cp)
    rest()
    score_t.wait_recv()

    def teacher(i, carry):
        at = pl.ds(pl.multiple_of(i * 32, 32), 32)
        t = jnp.tanh((town[at, :] + trecv[at, :].astype(F32)) / CAP)
        w = jnp.exp((CAP / 2) * t).astype(BF16)
        wts[at, :] = w
        w = w.astype(F32)
        total = jnp.sum(w, axis=1, keepdims=True)
        cross = CAP * jnp.sum(w * bnd[at, :], axis=1, keepdims=True)
        stat[at, :] = jnp.where(lane == 0, total, jnp.where(lane == 3, cross, stat[at, :]))
        return carry

    lax.fori_loop(0, HALF // 32, teacher, 0)

    def everywhere(slots, me, n, peer, value, ssem, rsem):
        slots[pl.ds(me, 1)] = value[None]
        copies = [send(slots.at[me], slots.at[me], ssem.at[k - 1], rsem.at[k - 1], peer(k)) for k in range(1, n)]
        arrive(copies)
        return jnp.sum(slots[...], axis=0), copies

    part = jnp.transpose(stat[...])[0:8, :]
    part, stat_x = everywhere(sx, x, NX, xp, part, xs, xr)
    part, stat_y = everywhere(sy, y, NY, yp, part, ys, yr)
    part, stat_z = everywhere(sz, z, NZ, zp, part, zs, zr)
    statc[...] = jnp.transpose(jnp.concatenate([part, jnp.ones((120, HALF), F32)], axis=0))

    per_token = 2.0 * (jnp.log(part[1:2]) - 0.5 * part[3:4] / part[0:1]) + 0.5 * (jnp.log(part[2:3]) - part[4:5])
    lost = jnp.sum(maskrow * per_token, axis=1, keepdims=True)
    lbuf[...] = jnp.broadcast_to(lost, (8, 128))
    loss_c = send(lbuf, lrecv, cs.at[2], cr.at[2], cp)

    def grad(i, carry):
        at = pl.ds(pl.multiple_of(i * 32, 32), 32)
        m = mskc[at, 0:1]
        b, s = bnd[at, :], soft[at, :]
        rt, rs, rh = m / statc[at, 0:1], m / statc[at, 1:2], 0.5 * m / statc[at, 2:3]
        g = s * (rs + rh * s) - wts[at, :].astype(F32) * rt
        g = g - jnp.where(columnf == labc[at, 0:1], 0.5 * m, 0.0)
        gfull[c, at, :] = (g * (1.0 - b * b)).astype(BF16)
        return carry

    lax.fori_loop(0, HALF // 32, grad, 0)
    grad_c = send(gfull.at[c], gfull.at[c], cs.at[3], cr.at[3], cp)
    grad_c.wait_recv()

    def product(first, width):
        out = []
        for h in range(2):
            out.append(jnp.dot(gfull[h], sev[:, first : first + width], preferred_element_type=F32).astype(BF16))
        return out

    def fill(dst, first, width, at):
        for h, block in enumerate(product(first, width)):
            dst[2 * h : 2 * h + 2, :, :, at : at + width] = block.reshape(2, 8, 16, width)

    for n in range(0, CXY, 256):
        fill(gx, n, 256, n)
        fill(gx, CA + n, 256, CXY + n)
    out_x = [send(gx.at[xi(k)], rx.at[k - 1], x1s.at[k - 1], x1r.at[k - 1], xp(k)) for k in range(1, NX)]
    fill(gy, CXY, CYX, 0)
    out_y = [send(gy.at[:, yi(k)], ry.at[k - 1], y1s.at[k - 1], y1r.at[k - 1], yp(k)) for k in range(1, NY)]
    fill(gz, CA + CXY, CYX, 0)
    out_z = [send(gz.at[:, zi(k)], rz.at[k - 1], z1s.at[k - 1], z1r.at[k - 1], zp(k)) for k in range(1, NZ)]

    arrive(out_x)
    for j in range(8):
        total = gx[x, j].astype(F32)
        for k in range(NX - 1):
            total = total + rx[k, j].astype(F32)
        total = total.astype(BF16)
        hxy[j] = total[:, :CXY]
        hxz[j] = total[:, CXY:]
    out_xy = [send(hxy.at[yi(k)], r2y.at[k - 1], y2s.at[k - 1], y2r.at[k - 1], yp(k)) for k in range(1, NY)]
    out_xz = [send(hxz.at[zi(k)], r2z.at[k - 1], z2s.at[k - 1], z2r.at[k - 1], zp(k)) for k in range(1, NZ)]
    arrive(out_y)
    for q in range(NX):
        total = gy[q, y].astype(F32)
        for k in range(NY - 1):
            total = total + ry[k, q].astype(F32)
        hx2[q, 0] = total.astype(BF16)
    arrive(out_z)
    for q in range(NX):
        total = gz[q, z].astype(F32)
        for k in range(NZ - 1):
            total = total + rz[k, q].astype(F32)
        hx2[q, 1] = total.astype(BF16)
    out_yx = [send(hx2.at[xi(k)], r2x.at[k - 1], x2s.at[k - 1], x2r.at[k - 1], xp(k)) for k in range(1, NX)]

    arrive(out_xy)
    total = hxy[y].astype(F32)
    for k in range(NY - 1):
        total = total + r2y[k].astype(F32)
    ra[z, :, 0:CXY] = total.astype(BF16)
    arrive(out_xz)
    total = hxz[z].astype(F32)
    for k in range(NZ - 1):
        total = total + r2z[k].astype(F32)
    rb[y, :, 0:CXY] = total.astype(BF16)
    arrive(out_yx)
    for i, dst, me in ((0, ra, z), (1, rb, y)):
        total = hx2[x, i].astype(F32)
        for k in range(NX - 1):
            total = total + r2x[k, i].astype(F32)
        dst[me, :, CXY:CA] = total.astype(BF16)
    all_a = [send(ra.at[z], ra.at[z], az.at[k - 1], azr.at[k - 1], zp(k)) for k in range(1, NZ)]
    all_b = [send(rb.at[y], rb.at[y], by.at[k - 1], byr.at[k - 1], yp(k)) for k in range(1, NY)]
    arrive(all_a)
    outv[y, :, 0:CA] = jnp.sum(ra[...].astype(F32), axis=0).astype(BF16)
    spread_a = [
        send(outv.at[y, :, pl.ds(0, CA)], outv.at[y, :, pl.ds(0, CA)], ay.at[k - 1], ayr.at[k - 1], yp(k))
        for k in range(1, NY)
    ]
    arrive(all_b)
    outv[z, :, CA:DS] = jnp.sum(rb[...].astype(F32), axis=0).astype(BF16)
    spread_b = [
        send(outv.at[z, :, pl.ds(CA, CA)], outv.at[z, :, pl.ds(CA, CA)], bz.at[k - 1], bzr.at[k - 1], zp(k))
        for k in range(1, NZ)
    ]
    loss_c.wait_recv()
    count = jnp.sum(msk[...].astype(F32), keepdims=True)
    loss_ref[...] = (lbuf[0:1, 0:1] + lrecv[0:1, 0:1]) / jnp.maximum(count, 1.0)
    for group in (
        sgather, tgather, [score_s, score_t, loss_c, grad_c], stat_x, stat_y, stat_z,
        out_x, out_y, out_z, out_xy, out_xz, out_yx, all_a, all_b,
    ):
        leave(group)
    arrive(spread_a)
    arrive(spread_b)
    leave(spread_a)
    leave(spread_b)
    done = pltpu.make_async_copy(outv, out_ref, lsem.at[4])
    done.start()
    done.wait()


def shards(th, te, sh, se, labels, mask):
    hbm = pl.BlockSpec(memory_space=pl.ANY)
    vmem = pl.BlockSpec(memory_space=pltpu.VMEM)
    V = pltpu.VMEM

    def sems(n):
        return pltpu.SemaphoreType.DMA((n,))

    loss, grad = pl.pallas_call(
        body,
        out_shape=(jax.ShapeDtypeStruct((1, 1), F32), jax.ShapeDtypeStruct((8, 16, DS), BF16)),
        in_specs=[hbm, hbm, hbm, hbm, vmem, vmem],
        out_specs=(vmem, hbm),
        scratch_shapes=[
            V((NX, QUARTER, DT), BF16), V((NX, QUARTER, DS), BF16), V((VB, DT), BF16), V((VB, DS), BF16),
            V((HALF, VB), BF16), V((HALF, VB), BF16), V((HALF, VB), F32),
            V((HALF, VB), F32), V((HALF, VB), F32), V((HALF, VB), F32),
            V((HALF, VB), BF16), V((HALF, VB), F32), V((HALF, VB), F32),
            V((HALF, 128), F32), V((HALF, 128), F32), V((HALF, 128), F32), V((HALF, 128), F32),
            V((NX, 8, HALF), F32), V((NY, 8, HALF), F32), V((NZ, 8, HALF), F32),
            V((8, 128), F32), V((8, 128), F32),
            V((2, HALF, VB), BF16),
            V((NX, 8, 16, 2 * CXY), BF16), V((NX, 8, 16, CYX), BF16), V((NX, 8, 16, CYX), BF16),
            V((NX - 1, 8, 16, 2 * CXY), BF16), V((NY - 1, NX, 16, CYX), BF16), V((NZ - 1, NX, 16, CYX), BF16),
            V((8, 16, CXY), BF16), V((8, 16, CXY), BF16), V((NY - 1, 16, CXY), BF16), V((NZ - 1, 16, CXY), BF16),
            V((NX, 2, 16, CYX), BF16), V((NX - 1, 2, 16, CYX), BF16),
            V((16, CA), BF16), V((16, CA), BF16), V((NZ, 16, CA), BF16), V((NY, 16, CA), BF16),
            V((8, 16, DS), BF16),
            sems(5), sems(8), sems(8), sems(4), sems(4),
            sems(3), sems(3), sems(7), sems(7), sems(7), sems(7),
            sems(3), sems(3), sems(7), sems(7), sems(7), sems(7),
            sems(3), sems(3), sems(7), sems(7), sems(7), sems(7),
            sems(7), sems(7), sems(7), sems(7), sems(7), sems(7), sems(7), sems(7),
        ],
        compiler_params=pltpu.CompilerParams(
            collective_id=0, has_side_effects=True, vmem_limit_bytes=56 * 2**20
        ),
        name="distill",
    )(th, te, sh, se, labels.reshape(2, HALF), mask.reshape(2, HALF))
    return loss.reshape(()), grad.reshape(QUARTER, DS)


def solution(mesh):
    placed = (
        P("rep", "inner"),
        P(("vocab", "rep"), "inner"),
        P("rep", "inner"),
        P(("vocab", "rep"), "inner"),
        P(),
        P(),
    )
    return jax.shard_map(
        shards, mesh=mesh, in_specs=placed, out_specs=(P(), P("rep", "inner")), check_vma=False
    )
```

```python
import jax
import jax.numpy as jnp
from jax import lax
from jax.experimental import pallas as pl
from jax.experimental.pallas import tpu as pltpu
from jax.sharding import PartitionSpec as P

MESH = pl.DeviceIdType.MESH
CAP = 30.0
NX, NY, NZ = 4, 8, 8
TOK, DT, DS, VB = 512, 2304, 1792, 512
HALF = TOK // 2
QUARTER = TOK // NX
CX = 256
CHUNKS = ((0, 512, 384), (896, 384, 512))
F32, BF16 = jnp.float32, jnp.bfloat16
STUDENT_PARTS = ((0, 512, "y", 0, 0), (512, 512, "z", 0, 1), (1024, 384, "y", 1, 1), (1408, 384, "z", 1, 0))
TEACHER_PARTS = ((0, 640, "y", 0, 1), (640, 640, "z", 0, 0), (1280, 512, "y", 1, 0), (1792, 512, "z", 1, 1))
FAR_FIRST = (4, 3, 5, 2, 6, 1, 7)


class Fixed:
    def __init__(self, ref, index):
        self.ref, self.index = ref, index

    @property
    def at(self):
        return self

    def __getitem__(self, _):
        return self.ref.at[self.index]


class Same(Fixed):
    def __init__(self, ref):
        self.ref = ref

    def __getitem__(self, _):
        return self.ref


def nt(left, right):
    return lax.dot_general(left, right, (((1,), (1,)), ((), ())), preferred_element_type=F32)


def body(
    th, te, sh, se, lab, msk, loss_ref, out_ref,
    thg, shg, tev, sev,
    tsend, trecv, town, ssend, srecv, sown,
    wts, soft, bnd, labc, mskc, stat, statc, sx, sy, sz, ux, uy, uz, lbuf, lrecv,
    gfull, outv,
    lsem, gs, gr, cs, cr, xs, xr, ys, yr, zs, zr, uxs, uxr, uys, uyr, uzs, uzr, x1s, x1r, y1s, y1r, z1s, z1r,
    x2s, x2r, x3s, x3r, y2s, y2r, z2s, z2r, azs, azr, bys, byr, ays, ayr, bzs, bzr, *rest_bufs,
):
    bufs = [rest_bufs[16 * i : 16 * i + 16] for i in range(len(CHUNKS))]
    v = lax.axis_index("vocab")
    c = lax.axis_index("inner")
    x = lax.axis_index("rep")
    z, y = v // NY, v % NY

    def xi(k):
        return lax.rem(x + k, NX)

    def yi(k):
        return lax.rem(y + k, NY)

    def zi(k):
        return lax.rem(z + k, NZ)

    def xp(k):
        return (v, c, xi(k))

    def yp(k):
        return (z * NY + yi(k), c, x)

    def zp(k):
        return (zi(k) * NY + y, c, x)

    cp = (v, 1 - c, x)
    flip = (x, x + 1 - 2 * (x % 2), x + 2 - 4 * (x // 2), 3 - x)
    odd = x % 2

    def send(src, dst, ssem, rsem, to):
        copy = pltpu.make_async_remote_copy(
            src_ref=src, dst_ref=dst, send_sem=ssem, recv_sem=rsem, device_id=to, device_id_type=MESH
        )
        copy.start()
        return copy

    def arrive(copies):
        for copy in copies:
            copy.wait_recv()

    def leave(copies):
        for copy in copies:
            copy.wait_send()

    loads = [
        pltpu.make_async_copy(se, sev, lsem.at[0]),
        pltpu.make_async_copy(te, tev, lsem.at[1]),
        pltpu.make_async_copy(sh, shg.at[0], lsem.at[2]),
        pltpu.make_async_copy(th, thg.at[0], lsem.at[3]),
    ]
    for load in loads:
        load.start()

    barrier = pltpu.get_barrier_semaphore()
    others = [xp(k) for k in (2, 1, 3)] + [cp]
    others = [p(k) for k in FAR_FIRST for p in (yp, zp)] + others
    for other in others:
        pl.semaphore_signal(barrier, inc=1, device_id=other, device_id_type=MESH)
    pl.semaphore_wait(barrier, len(others))

    def gather(source, buffer, parts, base):
        out = []
        for p, (first, width, order, shift_y, shift_z) in enumerate(parts):
            cols = pl.ds(first, width)
            bit_y, bit_z = (y + shift_y) % 2, (z + shift_z) % 2
            pair_y, pair_z = yp(NY + 1 - 2 * bit_y), zp(NZ + 1 - 2 * bit_z)
            if order == "y":
                bf, bs, pf, ps = bit_y, bit_z, pair_y, pair_z
            else:
                bf, bs, pf, ps = bit_z, bit_y, pair_z, pair_y
            i = base + p
            copies = [
                send(source.at[:, bs, bf, :, cols], buffer.at[k, :, bs, bf, :, cols],
                     gs.at[i, k], gr.at[i, k], (v, c, flip[k]))
                for k in (2, 1, 3)
            ]

            def first_swap(copies=copies, i=i, bs=bs, bf=bf, cols=cols, pf=pf):
                arrive(copies)
                block = buffer.at[pl.ds(1, 3), :, bs, bf, :, cols]
                return send(block, block, gs.at[i, 0], gr.at[i, 0], pf)

            def second_swap(swapped, i=i, bs=bs, cols=cols, ps=ps):
                arrive([swapped])
                block = buffer.at[pl.ds(1, 3), :, bs, :, :, cols]
                return send(block, block, gs.at[i, 4], gr.at[i, 4], ps)

            gathers.extend(copies)
            out.append((first_swap, second_swap))
        return out

    gathers = []
    parts = gather(sh, shg, STUDENT_PARTS, 0) + gather(th, thg, TEACHER_PARTS, 4)

    def row(ref):
        whole = ref[...].astype(F32).reshape(1, TOK)
        return jnp.where(c == 0, whole[:, :HALF], whole[:, HALF:])

    labc[...] = jnp.transpose(jnp.broadcast_to(row(lab), (128, HALF)))
    maskrow = row(msk)
    mskc[...] = jnp.transpose(jnp.broadcast_to(maskrow, (128, HALF)))

    once, twice = [], []
    for p in range(4):
        once.append(parts[p][0]())
    for p in range(4):
        twice.append(parts[p][1](once[p]))
        once.append(parts[4 + p][0]())
    for p in range(4, 8):
        twice.append(parts[p][1](once[p]))

    def scores(gathered, table, depth, sent, own):
        def block(which, n, into):
            pair = which + x // 2 - 2 * which * (x // 2)
            rows = gathered[pl.ds(2 * pair, 2)].reshape(HALF, depth)
            out = nt(rows, table[n : n + 256, :]).astype(into.dtype)
            into[odd, :, n : n + 256] = out[:QUARTER]
            into[1 - odd, :, n : n + 256] = out[QUARTER:]

        for n in range(0, VB, 256):
            block(1 - c, n, sent)

        def rest():
            for n in range(0, VB, 256):
                block(c, n, own)

        return rest

    loads[0].wait()
    loads[2].wait()
    arrive(twice[:4])
    rest = scores(shg, sev, DS, ssend, sown)
    score_s = send(ssend, srecv, cs.at[0], cr.at[0], cp)
    rest()

    score_s.wait_recv()
    lane = lax.broadcasted_iota(jnp.int32, (32, 128), 1)
    column = lax.broadcasted_iota(jnp.int32, (32, VB), 1) + (v * NX + x) * VB
    columnf = column.astype(F32)

    def student(i, carry):
        at = pl.ds(pl.multiple_of(i * 32, 32), 32)
        h, w = i // 4, pl.ds(pl.multiple_of((i % 4) * 32, 32), 32)
        b = jnp.tanh((sown[h, w, :] + srecv[h, w, :]) / CAP)
        s = jnp.exp((CAP / 2) * b)
        bnd[at, :] = b
        soft[at, :] = s
        hit = jnp.where(columnf == labc[at, 0:1], b, 0.0)
        total = jnp.sum(s, axis=1, keepdims=True)
        hard = jnp.sum(s * s, axis=1, keepdims=True)
        label = CAP * jnp.sum(hit, axis=1, keepdims=True)
        stat[at, :] = jnp.where(lane == 1, total, jnp.where(lane == 2, hard, jnp.where(lane == 4, label, 0.0)))
        return carry

    lax.fori_loop(0, HALF // 32, student, 0)

    loads[1].wait()
    loads[3].wait()
    arrive(twice[4:])
    rest = scores(thg, tev, DT, tsend, town)
    score_t = send(tsend, trecv, cs.at[1], cr.at[1], cp)
    rest()
    score_t.wait_recv()

    def teacher(i, carry):
        at = pl.ds(pl.multiple_of(i * 32, 32), 32)
        h, w = i // 4, pl.ds(pl.multiple_of((i % 4) * 32, 32), 32)
        t = jnp.tanh((town[h, w, :] + trecv[h, w, :].astype(F32)) / CAP)
        e = jnp.exp((CAP / 2) * t).astype(BF16)
        wts[at, :] = e
        e = e.astype(F32)
        total = jnp.sum(e, axis=1, keepdims=True)
        cross = CAP * jnp.sum(e * bnd[at, :], axis=1, keepdims=True)
        stat[at, :] = jnp.where(lane == 0, total, jnp.where(lane == 3, cross, stat[at, :]))
        return carry

    lax.fori_loop(0, HALF // 32, teacher, 0)

    def spread(slots, me, order, peer, value, ssem, rsem):
        slots[pl.ds(me, 1)] = value[None]
        return [send(slots.at[me], slots.at[me], ssem.at[k - 1], rsem.at[k - 1], peer(k)) for k in order]

    def collect(slots, copies):
        arrive(copies)
        stats.extend(copies)
        return jnp.sum(slots[...], axis=0)

    stats = []
    low, high = jnp.transpose(stat[0:QUARTER, :]), jnp.transpose(stat[QUARTER:HALF, :])

    def tile(*rows):
        both = [piece[r : r + 1] for r in rows for piece in (low, high)]
        return jnp.concatenate(both + [jnp.zeros((8 - len(both), 128), F32)], axis=0)

    sent = spread(sx, x, (2, 1, 3), xp, tile(0, 1, 2), xs, xr)
    aux = spread(ux, x, (2, 1, 3), xp, tile(3, 4), uxs, uxr)
    part = collect(sx, sent)
    part = collect(sy, spread(sy, y, FAR_FIRST, yp, part, ys, yr))
    part = collect(sz, spread(sz, z, FAR_FIRST, zp, part, zs, zr))
    statc[...] = jnp.transpose(jnp.concatenate([part, jnp.ones((120, 128), F32)], axis=0))

    for h in range(2):
        def grad(i, carry, h=h):
            at = pl.ds(pl.multiple_of(h * QUARTER + i * 32, 32), 32)
            w = pl.ds(pl.multiple_of(i * 32, 32), 32)
            m = mskc[at, 0:1]
            b, s = bnd[at, :], soft[at, :]
            rt, rs = m / statc[w, h : h + 1], m / statc[w, 2 + h : 3 + h]
            rh = 0.5 * m / statc[w, 4 + h : 5 + h]
            g = s * (rs + rh * s) - wts[at, :].astype(F32) * rt
            g = g - jnp.where(columnf == labc[at, 0:1], 0.5 * m, 0.0)
            gfull[c, at, :] = (g * (1.0 - b * b)).astype(BF16)
            return carry

        lax.fori_loop(0, QUARTER // 32, grad, 0)
    grad_c = send(gfull.at[c], gfull.at[c], cs.at[3], cr.at[3], cp)
    aux = spread(uy, y, FAR_FIRST, yp, collect(ux, aux), uys, uyr)

    def reduction(index, first, wide_a, wide_b):
        gx, gy, gz, rx, ry, rz, hxy, hxz, r2y, r2z, hy, hz, ry2, rz2, ra, rb = bufs[index]
        n = index
        rest_a, rest_b = wide_a - CX, wide_b - CX
        mid, last = first + wide_a, first + wide_a + wide_b

        def fill(which):
            def one(dst, at, start, width):
                block = jnp.dot(gfull[which], sev[:, start : start + width], preferred_element_type=F32)
                dst[pl.ds(2 * which, 2), :, :, at : at + width] = block.astype(BF16).reshape(2, 8, 16, width)

            one(gx, 0, first, CX)
            one(gx, CX, mid, CX)
            one(gy, 0, first + CX, rest_a)
            one(gz, 0, mid + CX, rest_b)

        def over(src, dst, order, peer, index_of, ssem, rsem):
            return [
                send(src(index_of(k)), dst.at[k - 1], ssem.at[n, k - 1], rsem.at[n, k - 1], peer(k)) for k in order
            ]

        def total(mine, received):
            out = mine.astype(F32)
            for block in received:
                out = out + block.astype(F32)
            return out.astype(BF16)

        def stage1():
            out_x = over(lambda q: gx.at[q], rx, (2, 1, 3), xp, xi, x1s, x1r)
            out_y = over(lambda j: gy.at[:, j], ry, FAR_FIRST, yp, yi, y1s, y1r)
            out_z = over(lambda j: gz.at[:, j], rz, FAR_FIRST, zp, zi, z1s, z1r)
            done.extend(out_x + out_y + out_z)
            return out_x, out_y, out_z

        def stage2(sent):
            arrive(sent[1])
            for q in range(NX):
                hy[q] = total(gy[q, y], [ry[k, q] for k in range(NY - 1)])
            out_yx = over(lambda q: hy.at[q], ry2, (2, 1, 3), xp, xi, x2s, x2r)
            arrive(sent[2])
            for q in range(NX):
                hz[q] = total(gz[q, z], [rz[k, q] for k in range(NZ - 1)])
            out_zx = over(lambda q: hz.at[q], rz2, (2, 1, 3), xp, xi, x3s, x3r)
            arrive(sent[0])
            for j in range(8):
                both = total(gx[x, j], [rx[k, j] for k in range(NX - 1)])
                hxy[j] = both[:, :CX]
                hxz[j] = both[:, CX:]
            out_xy = over(lambda j: hxy.at[j], r2y, FAR_FIRST, yp, yi, y2s, y2r)
            out_xz = over(lambda j: hxz.at[j], r2z, FAR_FIRST, zp, zi, z2s, z2r)
            done.extend(out_yx + out_zx + out_xy + out_xz)
            return out_yx, out_zx, out_xy, out_xz

        def stage3(sent):
            arrive(sent[0])
            ra[z, :, CX:wide_a] = total(hy[x], [ry2[k] for k in range(NX - 1)])
            arrive(sent[1])
            rb[y, :, CX:wide_b] = total(hz[x], [rz2[k] for k in range(NX - 1)])
            arrive(sent[2])
            ra[z, :, 0:CX] = total(hxy[y], [r2y[k] for k in range(NY - 1)])
            all_a = over(lambda _: ra.at[z], Fixed(ra, z), FAR_FIRST, zp, zi, azs, azr)
            arrive(sent[3])
            rb[y, :, 0:CX] = total(hxz[z], [r2z[k] for k in range(NZ - 1)])
            all_b = over(lambda _: rb.at[y], Fixed(rb, y), FAR_FIRST, yp, yi, bys, byr)
            done.extend(all_a + all_b)
            return all_a, all_b

        def stage4(sent):
            cols_a, cols_b = pl.ds(first, wide_a), pl.ds(mid, wide_b)
            arrive(sent[0])
            outv[y, :, cols_a] = jnp.sum(ra[...].astype(F32), axis=0).astype(BF16)
            here = outv.at[y, :, cols_a]
            out_a = over(lambda _: here, Same(here), FAR_FIRST, yp, yi, ays, ayr)
            arrive(sent[1])
            outv[z, :, cols_b] = jnp.sum(rb[...].astype(F32), axis=0).astype(BF16)
            there = outv.at[z, :, cols_b]
            out_b = over(lambda _: there, Same(there), FAR_FIRST, zp, zi, bzs, bzr)
            return out_a + out_b

        return fill, stage1, stage2, stage3, stage4

    done = []
    chunks = [reduction(i, *chunk) for i, chunk in enumerate(CHUNKS)]
    for fill, *_ in chunks[:1]:
        fill(c)
    grad_c.wait_recv()
    pipe = []
    for i, chunk in enumerate(chunks):
        if i > 0:
            chunk[0](c)
        chunk[0](1 - c)
        pipe.append(chunk[1]())
    aux = spread(uz, z, FAR_FIRST, zp, collect(uy, aux), uzs, uzr)
    pipe = [chunk[2](sent) for chunk, sent in zip(chunks, pipe)]
    rest_of = collect(uz, aux)
    lost = jnp.zeros((1, 1), F32)
    for h in range(2):
        per_token = 2.0 * (jnp.log(part[2 + h : 3 + h]) - 0.5 * rest_of[h : h + 1] / part[h : h + 1])
        per_token = per_token + 0.5 * (jnp.log(part[4 + h : 5 + h]) - rest_of[2 + h : 3 + h])
        owned = maskrow[:, h * QUARTER : (h + 1) * QUARTER]
        lost = lost + jnp.sum(owned * per_token, axis=1, keepdims=True)
    lbuf[...] = jnp.broadcast_to(lost, (8, 128))
    loss_c = send(lbuf, lrecv, cs.at[2], cr.at[2], cp)
    pipe = [chunk[3](sent) for chunk, sent in zip(chunks, pipe)]
    pipe = [chunk[4](sent) for chunk, sent in zip(chunks, pipe)]
    loss_c.wait_recv()
    count = jnp.sum(msk[...].astype(F32).reshape(1, TOK), axis=1, keepdims=True)
    loss_ref[...] = (lbuf[0:1, 0:1] + lrecv[0:1, 0:1]) / jnp.maximum(count, 1.0)
    for group in (gathers, once, twice, [score_s, score_t, loss_c, grad_c], stats, done):
        leave(group)
    for copies in pipe:
        arrive(copies)
    for copies in pipe:
        leave(copies)
    result = pltpu.make_async_copy(outv, out_ref, lsem.at[4])
    result.start()
    result.wait()


def shards(th, te, sh, se, labels, mask):
    hbm = pl.BlockSpec(memory_space=pl.ANY)
    vmem = pl.BlockSpec(memory_space=pltpu.VMEM)
    V = pltpu.VMEM

    def sems(n):
        return pltpu.SemaphoreType.DMA((n,))

    def each(n):
        return pltpu.SemaphoreType.DMA((len(CHUNKS), n))

    loss, grad = pl.pallas_call(
        body,
        out_shape=(jax.ShapeDtypeStruct((1, 1), F32), jax.ShapeDtypeStruct((8, 16, DS), BF16)),
        in_specs=[hbm, hbm, hbm, hbm, vmem, vmem],
        out_specs=(vmem, hbm),
        scratch_shapes=[
            V((NX, 2, 2, 2, 16, DT), BF16), V((NX, 2, 2, 2, 16, DS), BF16), V((VB, DT), BF16), V((VB, DS), BF16),
            V((2, QUARTER, VB), BF16), V((2, QUARTER, VB), BF16), V((2, QUARTER, VB), F32),
            V((2, QUARTER, VB), F32), V((2, QUARTER, VB), F32), V((2, QUARTER, VB), F32),
            V((HALF, VB), BF16), V((HALF, VB), F32), V((HALF, VB), F32),
            V((HALF, 128), F32), V((HALF, 128), F32), V((HALF, 128), F32), V((QUARTER, 128), F32),
            V((NX, 8, 128), F32), V((NY, 8, 128), F32), V((NZ, 8, 128), F32),
            V((NX, 8, 128), F32), V((NY, 8, 128), F32), V((NZ, 8, 128), F32),
            V((8, 128), F32), V((8, 128), F32),
            V((2, HALF, VB), BF16),
            V((8, 16, DS), BF16),
            sems(5), pltpu.SemaphoreType.DMA((8, 5)), pltpu.SemaphoreType.DMA((8, 5)), sems(4), sems(4),
            sems(3), sems(3), sems(7), sems(7), sems(7), sems(7),
            sems(3), sems(3), sems(7), sems(7), sems(7), sems(7),
            each(3), each(3), each(7), each(7), each(7), each(7),
            each(3), each(3), each(3), each(3), each(7), each(7), each(7), each(7),
            each(7), each(7), each(7), each(7), each(7), each(7), each(7), each(7),
            *[
                V(shape, BF16)
                for _, wide_a, wide_b in CHUNKS
                for ca, cb in ((wide_a - CX, wide_b - CX),)
                for shape in (
                    (NX, 8, 16, 2 * CX), (NX, 8, 16, ca), (NX, 8, 16, cb),
                    (NX - 1, 8, 16, 2 * CX), (NY - 1, NX, 16, ca), (NZ - 1, NX, 16, cb),
                    (8, 16, CX), (8, 16, CX), (NY - 1, 16, CX), (NZ - 1, 16, CX),
                    (NX, 16, ca), (NX, 16, cb), (NX - 1, 16, ca), (NX - 1, 16, cb),
                    (NZ, 16, wide_a), (NY, 16, wide_b),
                )
            ],
        ],
        compiler_params=pltpu.CompilerParams(
            collective_id=0, has_side_effects=True, vmem_limit_bytes=56 * 2**20
        ),
        name="distill",
    )(th.reshape(2, 2, 2, 16, DT), te, sh.reshape(2, 2, 2, 16, DS), se, labels, mask)
    return loss.reshape(()), grad.reshape(QUARTER, DS)


def solution(mesh):
    placed = (
        P("rep", "inner"),
        P(("vocab", "rep"), "inner"),
        P("rep", "inner"),
        P(("vocab", "rep"), "inner"),
        P(),
        P(),
    )
    return jax.shard_map(
        shards, mesh=mesh, in_specs=placed, out_specs=(P(), P("rep", "inner")), check_vma=False
    )
```

```python
import jax
import jax.numpy as jnp
from jax import lax
from jax.experimental import pallas as pl
from jax.experimental.pallas import tpu as pltpu
from jax.sharding import PartitionSpec as P

MESH = pl.DeviceIdType.MESH
CAP = 30.0
NX, NY, NZ = 4, 8, 8
TOK, DT, DS, VB = 512, 2304, 1792, 512
HALF = TOK // 2
QUARTER = TOK // NX
CX = 256
CHUNKS = ((0, 512, 384), (896, 384, 512))
F32, BF16 = jnp.float32, jnp.bfloat16
STUDENT_PARTS = ((0, 512, "y", 0, 0), (512, 512, "z", 0, 1), (1024, 384, "y", 1, 1), (1408, 384, "z", 1, 0))
TEACHER_PARTS = ((0, 384, "y", 0, 1), (384, 384, "z", 0, 0), (768, 384, "y", 1, 0), (1152, 384, "z", 1, 1))
TEACHER_REST = (1536, 768)
FAR_FIRST = (4, 3, 5, 2, 6, 1, 7)


class Fixed:
    def __init__(self, ref, index):
        self.ref, self.index = ref, index

    @property
    def at(self):
        return self

    def __getitem__(self, _):
        return self.ref.at[self.index]


class Same(Fixed):
    def __init__(self, ref):
        self.ref = ref

    def __getitem__(self, _):
        return self.ref


def nt(left, right):
    return lax.dot_general(left, right, (((1,), (1,)), ((), ())), preferred_element_type=F32)


def body(
    th, te, sh, se, lab, msk, loss_ref, out_ref,
    thg, shg, tev, sev,
    tsend, trecv, town, ssend, srecv, sown,
    wts, soft, bnd, labc, mskc, stat, statc, sx, sy, sz, ux, uy, uz, lbuf, lrecv,
    gfull, outv,
    lsem, gs, gr, cs, cr, xs, xr, ys, yr, zs, zr, uxs, uxr, uys, uyr, uzs, uzr, x1s, x1r, y1s, y1r, z1s, z1r,
    x2s, x2r, x3s, x3r, y2s, y2r, z2s, z2r, azs, azr, bys, byr, ays, ayr, bzs, bzr, *rest_bufs,
):
    bufs = [rest_bufs[16 * i : 16 * i + 16] for i in range(len(CHUNKS))]
    v = lax.axis_index("vocab")
    c = lax.axis_index("inner")
    x = lax.axis_index("rep")
    z, y = v // NY, v % NY

    def xi(k):
        return lax.rem(x + k, NX)

    def yi(k):
        return lax.rem(y + k, NY)

    def zi(k):
        return lax.rem(z + k, NZ)

    def xp(k):
        return (v, c, xi(k))

    def yp(k):
        return (z * NY + yi(k), c, x)

    def zp(k):
        return (zi(k) * NY + y, c, x)

    cp = (v, 1 - c, x)
    flip = (x, x + 1 - 2 * (x % 2), x + 2 - 4 * (x // 2), 3 - x)
    odd = x % 2

    def send(src, dst, ssem, rsem, to):
        copy = pltpu.make_async_remote_copy(
            src_ref=src, dst_ref=dst, send_sem=ssem, recv_sem=rsem, device_id=to, device_id_type=MESH
        )
        copy.start()
        return copy

    def arrive(copies):
        for copy in copies:
            copy.wait_recv()

    def leave(copies):
        for copy in copies:
            copy.wait_send()

    loads = [
        pltpu.make_async_copy(se, sev, lsem.at[0]),
        pltpu.make_async_copy(te, tev, lsem.at[1]),
        pltpu.make_async_copy(sh, shg.at[0], lsem.at[2]),
        pltpu.make_async_copy(th, thg.at[0], lsem.at[3]),
    ]
    for load in loads:
        load.start()

    barrier = pltpu.get_barrier_semaphore()
    others = [xp(k) for k in (2, 1, 3)] + [cp]
    others = [p(k) for k in FAR_FIRST for p in (yp, zp)] + others
    for other in others:
        pl.semaphore_signal(barrier, inc=1, device_id=other, device_id_type=MESH)
    pl.semaphore_wait(barrier, len(others))

    def gather(source, buffer, parts, base):
        out = []
        for p, (first, width, order, shift_y, shift_z) in enumerate(parts):
            cols = pl.ds(first, width)
            bit_y, bit_z = (y + shift_y) % 2, (z + shift_z) % 2
            pair_y, pair_z = yp(NY + 1 - 2 * bit_y), zp(NZ + 1 - 2 * bit_z)
            if order == "y":
                bf, bs, pf, ps = bit_y, bit_z, pair_y, pair_z
            else:
                bf, bs, pf, ps = bit_z, bit_y, pair_z, pair_y
            i = base + p
            copies = [
                send(source.at[:, bs, bf, :, cols], buffer.at[k, :, bs, bf, :, cols],
                     gs.at[i, k], gr.at[i, k], (v, c, flip[k]))
                for k in (2, 1, 3)
            ]

            def first_swap(copies=copies, i=i, bs=bs, bf=bf, cols=cols, pf=pf):
                arrive(copies)
                block = buffer.at[pl.ds(1, 3), :, bs, bf, :, cols]
                return send(block, block, gs.at[i, 0], gr.at[i, 0], pf)

            def second_swap(swapped, i=i, bs=bs, cols=cols, ps=ps):
                arrive([swapped])
                block = buffer.at[pl.ds(1, 3), :, bs, :, :, cols]
                return send(block, block, gs.at[i, 4], gr.at[i, 4], ps)

            gathers.extend(copies)
            out.append((first_swap, second_swap))
        return out

    gathers = []
    parts = gather(sh, shg, STUDENT_PARTS, 0) + gather(th, thg, TEACHER_PARTS, 4)

    def row(ref):
        whole = ref[...].astype(F32).reshape(1, TOK)
        return jnp.where(c == 0, whole[:, :HALF], whole[:, HALF:])

    labc[...] = jnp.transpose(jnp.broadcast_to(row(lab), (128, HALF)))
    maskrow = row(msk)
    mskc[...] = jnp.transpose(jnp.broadcast_to(maskrow, (128, HALF)))

    once, twice = [], []
    for p in range(4):
        once.append(parts[p][0]())
    for p in range(4):
        twice.append(parts[p][1](once[p]))
        once.append(parts[4 + p][0]())
    cols = pl.ds(*TEACHER_REST)
    alone = [
        send(th.at[w, :, :, :, cols], thg.at[k, w, :, :, :, cols], gs.at[8 + w, k], gr.at[8 + w, k], (v, c, flip[k]))
        for w in range(2)
        for k in (2, 1, 3)
    ]
    for p in range(4, 8):
        twice.append(parts[p][1](once[p]))

    def scores(gathered, table, depth, sent, own):
        def block(which, n, into):
            pair = which + x // 2 - 2 * which * (x // 2)
            rows = gathered[pl.ds(2 * pair, 2)].reshape(HALF, depth)
            out = nt(rows, table[n : n + 256, :]).astype(into.dtype)
            into[odd, :, n : n + 256] = out[:QUARTER]
            into[1 - odd, :, n : n + 256] = out[QUARTER:]

        for n in range(0, VB, 256):
            block(1 - c, n, sent)

        def rest():
            for n in range(0, VB, 256):
                block(c, n, own)

        return rest

    loads[0].wait()
    loads[2].wait()
    arrive(twice[:4])
    rest = scores(shg, sev, DS, ssend, sown)
    score_s = send(ssend, srecv, cs.at[0], cr.at[0], cp)
    rest()

    score_s.wait_recv()
    lane = lax.broadcasted_iota(jnp.int32, (32, 128), 1)
    column = lax.broadcasted_iota(jnp.int32, (32, VB), 1) + (v * NX + x) * VB
    columnf = column.astype(F32)

    def student(i, carry):
        at = pl.ds(pl.multiple_of(i * 32, 32), 32)
        h, w = i // 4, pl.ds(pl.multiple_of((i % 4) * 32, 32), 32)
        b = jnp.tanh((sown[h, w, :] + srecv[h, w, :]) / CAP)
        s = jnp.exp((CAP / 2) * b)
        bnd[at, :] = b
        soft[at, :] = s
        hit = jnp.where(columnf == labc[at, 0:1], b, 0.0)
        total = jnp.sum(s, axis=1, keepdims=True)
        hard = jnp.sum(s * s, axis=1, keepdims=True)
        label = CAP * jnp.sum(hit, axis=1, keepdims=True)
        stat[at, :] = jnp.where(lane == 1, total, jnp.where(lane == 2, hard, jnp.where(lane == 4, label, 0.0)))
        return carry

    lax.fori_loop(0, HALF // 32, student, 0)

    loads[1].wait()
    loads[3].wait()
    arrive(twice[4:])
    arrive(alone)
    rest = scores(thg, tev, DT, tsend, town)
    score_t = send(tsend, trecv, cs.at[1], cr.at[1], cp)
    rest()
    score_t.wait_recv()

    def teacher(i, carry):
        at = pl.ds(pl.multiple_of(i * 32, 32), 32)
        h, w = i // 4, pl.ds(pl.multiple_of((i % 4) * 32, 32), 32)
        t = jnp.tanh((town[h, w, :] + trecv[h, w, :].astype(F32)) / CAP)
        e = jnp.exp((CAP / 2) * t).astype(BF16)
        wts[at, :] = e
        e = e.astype(F32)
        total = jnp.sum(e, axis=1, keepdims=True)
        cross = CAP * jnp.sum(e * bnd[at, :], axis=1, keepdims=True)
        stat[at, :] = jnp.where(lane == 0, total, jnp.where(lane == 3, cross, stat[at, :]))
        return carry

    lax.fori_loop(0, HALF // 32, teacher, 0)

    def spread(slots, me, order, peer, value, ssem, rsem):
        slots[pl.ds(me, 1)] = value[None]
        return [send(slots.at[me], slots.at[me], ssem.at[k - 1], rsem.at[k - 1], peer(k)) for k in order]

    def collect(slots, copies):
        arrive(copies)
        stats.extend(copies)
        return jnp.sum(slots[...], axis=0)

    stats = []
    low, high = jnp.transpose(stat[0:QUARTER, :]), jnp.transpose(stat[QUARTER:HALF, :])

    def tile(*rows):
        both = [piece[r : r + 1] for r in rows for piece in (low, high)]
        return jnp.concatenate(both + [jnp.zeros((8 - len(both), 128), F32)], axis=0)

    sent = spread(sx, x, (2, 1, 3), xp, tile(0, 1, 2), xs, xr)
    aux = spread(ux, x, (2, 1, 3), xp, tile(3, 4), uxs, uxr)
    part = collect(sx, sent)
    part = collect(sy, spread(sy, y, FAR_FIRST, yp, part, ys, yr))
    part = collect(sz, spread(sz, z, FAR_FIRST, zp, part, zs, zr))
    statc[...] = jnp.transpose(jnp.concatenate([part, jnp.ones((120, 128), F32)], axis=0))

    for h in range(2):
        def grad(i, carry, h=h):
            at = pl.ds(pl.multiple_of(h * QUARTER + i * 32, 32), 32)
            w = pl.ds(pl.multiple_of(i * 32, 32), 32)
            m = mskc[at, 0:1]
            b, s = bnd[at, :], soft[at, :]
            rt, rs = m / statc[w, h : h + 1], m / statc[w, 2 + h : 3 + h]
            rh = 0.5 * m / statc[w, 4 + h : 5 + h]
            g = s * (rs + rh * s) - wts[at, :].astype(F32) * rt
            g = g - jnp.where(columnf == labc[at, 0:1], 0.5 * m, 0.0)
            gfull[c, at, :] = (g * (1.0 - b * b)).astype(BF16)
            return carry

        lax.fori_loop(0, QUARTER // 32, grad, 0)
    grad_c = send(gfull.at[c], gfull.at[c], cs.at[3], cr.at[3], cp)
    aux = spread(uy, y, FAR_FIRST, yp, collect(ux, aux), uys, uyr)

    def reduction(index, first, wide_a, wide_b):
        gx, gy, gz, rx, ry, rz, hxy, hxz, r2y, r2z, hy, hz, ry2, rz2, ra, rb = bufs[index]
        n = index
        rest_a, rest_b = wide_a - CX, wide_b - CX
        mid, last = first + wide_a, first + wide_a + wide_b

        def fill(which):
            def one(dst, at, start, width):
                block = jnp.dot(gfull[which], sev[:, start : start + width], preferred_element_type=F32)
                dst[pl.ds(2 * which, 2), :, :, at : at + width] = block.astype(BF16).reshape(2, 8, 16, width)

            one(gx, 0, first, CX)
            one(gx, CX, mid, CX)
            one(gy, 0, first + CX, rest_a)
            one(gz, 0, mid + CX, rest_b)

        def over(src, dst, order, peer, index_of, ssem, rsem):
            return [
                send(src(index_of(k)), dst.at[k - 1], ssem.at[n, k - 1], rsem.at[n, k - 1], peer(k)) for k in order
            ]

        def total(mine, received):
            out = mine.astype(F32)
            for block in received:
                out = out + block.astype(F32)
            return out.astype(BF16)

        def stage1():
            out_x = over(lambda q: gx.at[q], rx, (2, 1, 3), xp, xi, x1s, x1r)
            out_y = over(lambda j: gy.at[:, j], ry, FAR_FIRST, yp, yi, y1s, y1r)
            out_z = over(lambda j: gz.at[:, j], rz, FAR_FIRST, zp, zi, z1s, z1r)
            done.extend(out_x + out_y + out_z)
            return out_x, out_y, out_z

        def stage2(sent):
            arrive(sent[1])
            for q in range(NX):
                hy[q] = total(gy[q, y], [ry[k, q] for k in range(NY - 1)])
            out_yx = over(lambda q: hy.at[q], ry2, (2, 1, 3), xp, xi, x2s, x2r)
            arrive(sent[2])
            for q in range(NX):
                hz[q] = total(gz[q, z], [rz[k, q] for k in range(NZ - 1)])
            out_zx = over(lambda q: hz.at[q], rz2, (2, 1, 3), xp, xi, x3s, x3r)
            arrive(sent[0])
            for j in range(8):
                both = total(gx[x, j], [rx[k, j] for k in range(NX - 1)])
                hxy[j] = both[:, :CX]
                hxz[j] = both[:, CX:]
            out_xy = over(lambda j: hxy.at[j], r2y, FAR_FIRST, yp, yi, y2s, y2r)
            out_xz = over(lambda j: hxz.at[j], r2z, FAR_FIRST, zp, zi, z2s, z2r)
            done.extend(out_yx + out_zx + out_xy + out_xz)
            return out_yx, out_zx, out_xy, out_xz

        def stage3(sent):
            arrive(sent[0])
            ra[z, :, CX:wide_a] = total(hy[x], [ry2[k] for k in range(NX - 1)])
            arrive(sent[1])
            rb[y, :, CX:wide_b] = total(hz[x], [rz2[k] for k in range(NX - 1)])
            arrive(sent[2])
            ra[z, :, 0:CX] = total(hxy[y], [r2y[k] for k in range(NY - 1)])
            all_a = over(lambda _: ra.at[z], Fixed(ra, z), FAR_FIRST, zp, zi, azs, azr)
            arrive(sent[3])
            rb[y, :, 0:CX] = total(hxz[z], [r2z[k] for k in range(NZ - 1)])
            all_b = over(lambda _: rb.at[y], Fixed(rb, y), FAR_FIRST, yp, yi, bys, byr)
            done.extend(all_a + all_b)
            return all_a, all_b

        def stage4(sent):
            cols_a, cols_b = pl.ds(first, wide_a), pl.ds(mid, wide_b)
            arrive(sent[0])
            outv[y, :, cols_a] = jnp.sum(ra[...].astype(F32), axis=0).astype(BF16)
            here = outv.at[y, :, cols_a]
            out_a = over(lambda _: here, Same(here), FAR_FIRST, yp, yi, ays, ayr)
            arrive(sent[1])
            outv[z, :, cols_b] = jnp.sum(rb[...].astype(F32), axis=0).astype(BF16)
            there = outv.at[z, :, cols_b]
            out_b = over(lambda _: there, Same(there), FAR_FIRST, zp, zi, bzs, bzr)
            return out_a + out_b

        return fill, stage1, stage2, stage3, stage4

    done = []
    chunks = [reduction(i, *chunk) for i, chunk in enumerate(CHUNKS)]
    for fill, *_ in chunks[:1]:
        fill(c)
    grad_c.wait_recv()
    pipe = []
    for i, chunk in enumerate(chunks):
        if i > 0:
            chunk[0](c)
        chunk[0](1 - c)
        pipe.append(chunk[1]())
    aux = spread(uz, z, FAR_FIRST, zp, collect(uy, aux), uzs, uzr)
    pipe = [chunk[2](sent) for chunk, sent in zip(chunks, pipe)]
    rest_of = collect(uz, aux)
    lost = jnp.zeros((1, 1), F32)
    for h in range(2):
        per_token = 2.0 * (jnp.log(part[2 + h : 3 + h]) - 0.5 * rest_of[h : h + 1] / part[h : h + 1])
        per_token = per_token + 0.5 * (jnp.log(part[4 + h : 5 + h]) - rest_of[2 + h : 3 + h])
        owned = maskrow[:, h * QUARTER : (h + 1) * QUARTER]
        lost = lost + jnp.sum(owned * per_token, axis=1, keepdims=True)
    lbuf[...] = jnp.broadcast_to(lost, (8, 128))
    loss_c = send(lbuf, lrecv, cs.at[2], cr.at[2], cp)
    pipe = [chunk[3](sent) for chunk, sent in zip(chunks, pipe)]
    pipe = [chunk[4](sent) for chunk, sent in zip(chunks, pipe)]
    loss_c.wait_recv()
    count = jnp.sum(msk[...].astype(F32).reshape(1, TOK), axis=1, keepdims=True)
    loss_ref[...] = (lbuf[0:1, 0:1] + lrecv[0:1, 0:1]) / jnp.maximum(count, 1.0)
    for group in (gathers, alone, once, twice, [score_s, score_t, loss_c, grad_c], stats, done):
        leave(group)
    for copies in pipe:
        arrive(copies)
    for copies in pipe:
        leave(copies)
    result = pltpu.make_async_copy(outv, out_ref, lsem.at[4])
    result.start()
    result.wait()


def shards(th, te, sh, se, labels, mask):
    hbm = pl.BlockSpec(memory_space=pl.ANY)
    vmem = pl.BlockSpec(memory_space=pltpu.VMEM)
    V = pltpu.VMEM

    def sems(n):
        return pltpu.SemaphoreType.DMA((n,))

    def each(n):
        return pltpu.SemaphoreType.DMA((len(CHUNKS), n))

    loss, grad = pl.pallas_call(
        body,
        out_shape=(jax.ShapeDtypeStruct((1, 1), F32), jax.ShapeDtypeStruct((8, 16, DS), BF16)),
        in_specs=[hbm, hbm, hbm, hbm, vmem, vmem],
        out_specs=(vmem, hbm),
        scratch_shapes=[
            V((NX, 2, 2, 2, 16, DT), BF16), V((NX, 2, 2, 2, 16, DS), BF16), V((VB, DT), BF16), V((VB, DS), BF16),
            V((2, QUARTER, VB), BF16), V((2, QUARTER, VB), BF16), V((2, QUARTER, VB), F32),
            V((2, QUARTER, VB), F32), V((2, QUARTER, VB), F32), V((2, QUARTER, VB), F32),
            V((HALF, VB), BF16), V((HALF, VB), F32), V((HALF, VB), F32),
            V((HALF, 128), F32), V((HALF, 128), F32), V((HALF, 128), F32), V((QUARTER, 128), F32),
            V((NX, 8, 128), F32), V((NY, 8, 128), F32), V((NZ, 8, 128), F32),
            V((NX, 8, 128), F32), V((NY, 8, 128), F32), V((NZ, 8, 128), F32),
            V((8, 128), F32), V((8, 128), F32),
            V((2, HALF, VB), BF16),
            V((8, 16, DS), BF16),
            sems(5), pltpu.SemaphoreType.DMA((10, 5)), pltpu.SemaphoreType.DMA((10, 5)), sems(4), sems(4),
            sems(3), sems(3), sems(7), sems(7), sems(7), sems(7),
            sems(3), sems(3), sems(7), sems(7), sems(7), sems(7),
            each(3), each(3), each(7), each(7), each(7), each(7),
            each(3), each(3), each(3), each(3), each(7), each(7), each(7), each(7),
            each(7), each(7), each(7), each(7), each(7), each(7), each(7), each(7),
            *[
                V(shape, BF16)
                for _, wide_a, wide_b in CHUNKS
                for ca, cb in ((wide_a - CX, wide_b - CX),)
                for shape in (
                    (NX, 8, 16, 2 * CX), (NX, 8, 16, ca), (NX, 8, 16, cb),
                    (NX - 1, 8, 16, 2 * CX), (NY - 1, NX, 16, ca), (NZ - 1, NX, 16, cb),
                    (8, 16, CX), (8, 16, CX), (NY - 1, 16, CX), (NZ - 1, 16, CX),
                    (NX, 16, ca), (NX, 16, cb), (NX - 1, 16, ca), (NX - 1, 16, cb),
                    (NZ, 16, wide_a), (NY, 16, wide_b),
                )
            ],
        ],
        compiler_params=pltpu.CompilerParams(
            collective_id=0, has_side_effects=True, vmem_limit_bytes=56 * 2**20
        ),
        name="distill",
    )(th.reshape(2, 2, 2, 16, DT), te, sh.reshape(2, 2, 2, 16, DS), se, labels, mask)
    return loss.reshape(()), grad.reshape(QUARTER, DS)


def solution(mesh):
    placed = (
        P("rep", "inner"),
        P(("vocab", "rep"), "inner"),
        P("rep", "inner"),
        P(("vocab", "rep"), "inner"),
        P(),
        P(),
    )
    return jax.shard_map(
        shards, mesh=mesh, in_specs=placed, out_specs=(P(), P("rep", "inner")), check_vma=False
    )
```
